512 devices in a mesh: rows: 64 (over z, y_lo, x), feat: 8 (over y_hi, core).
Axes of the slice: x: 4, y: 8 (y_hi: 4, y_lo: 2; y = y_hi * 2 + y_lo), z: 8, core: 2. Of those that a mesh axis runs over, the one named last changes fastest.
Arguments:
- train_grads: bfloat16 [32768, 2, 128, 128], P('rows', None, 'feat'), may hold values from -0.03125 to 0.03125
- query_grads: bfloat16 [512, 2, 128, 128], P('rows', None, 'feat'), may hold values from -6 to 6
- out_inv: float32 [2, 128, 128], replicated, may hold values from -1 to 2, as said below
- in_inv: float32 [2, 128, 128], replicated, may hold values from -1 to 2, as said below
Outputs:
- scores: float32 [32768, 512], P('rows', 'feat')
The draws below stay inside these ranges and needn't reach their ends.
Inputs may be any that keep to these rules, and one draw needn't show every extreme that they name: `out_inv`: symmetric, with diagonal between 1 and 2 and small off-diagonal entries; positive definite. `in_inv`: symmetric, with diagonal between 1 and 2 and small off-diagonal entries; positive definite.
All inputs are finite; a program needn't handle non-finite values.
Results may differ from the reference program's by a relative error of at most 0.0029.
Values may be sent and summed in bfloat16 or wider, within the bound.
No kernel may reach another device: no remote copies, remote signals or barrier semaphores. Data moves between devices by JAX's collectives and lax.ppermute only.
A program may use at most 64 MiB of HBM per device.

```python
import jax
import jax.numpy as jnp
from jax import lax

OUT_W = 128
IN_W = 128
LAYERS = 2
ROW_DEV = 512
QUERIES = 512
TRAIN = 32768


def factor_draw(key, layers, width):
    key_off, key_diag = jax.random.split(key)
    raw = jax.random.uniform(key_off, (layers, width, width), jnp.float32, -1.0, 1.0)
    diag = jax.random.uniform(key_diag, (layers, width), jnp.float32, 1.0, 2.0)
    sym = 0.5 * (raw + jnp.swapaxes(raw, 1, 2)) * (0.9 / jnp.sqrt(jnp.float32(width)))
    eye = jnp.eye(width, dtype=jnp.float32)
    return sym * (1.0 - eye) + diag[:, :, None] * eye


def draw_out_inv(key, part):
    key = jax.random.fold_in(key, 11)
    return factor_draw(key, LAYERS, OUT_W)


def draw_in_inv(key, part):
    key = jax.random.fold_in(key, 23)
    return factor_draw(key, LAYERS, IN_W)


def block_scale(rng, dims, pieces, low, top_value):
    def one(position, shards_of):
        draws = jax.random.uniform(jax.random.fold_in(jax.random.fold_in(rng, 6), position), (shards_of,), jnp.float32, low / len(pieces), top_value / len(pieces))
        return jnp.repeat(jnp.exp(draws), dims[position] // shards_of).reshape((-1,) + (1,) * (len(dims) - position - 1))

    level = one(*pieces[0])
    for cut in pieces[1:]:
        level = level * one(*cut)
    return level


def noise(key, shape, spread, reach, pieces=(), kind=jnp.bfloat16):
    array = jax.random.normal(key, shape, jnp.float32) * spread
    if len(pieces) > 0:
        array = block_scale(key, shape, pieces, -0.22, 0.18) * array
    return jnp.clip(array, min=-reach, max=reach).astype(kind)


def setup_inputs(seed: int = 0) -> dict:
    arg_keys = jax.random.split(jax.random.key(seed), 5)
    return {
        "train_grads": noise(arg_keys[0], (TRAIN, LAYERS, OUT_W, IN_W), (LAYERS * OUT_W * IN_W) ** -0.5, 0.03125, ((0, 64), (2, 8))),
        "query_grads": noise(arg_keys[1], (QUERIES, LAYERS, OUT_W, IN_W), 1.0, 6.0, ((0, 64), (2, 8))),
        "out_inv": draw_out_inv(jax.random.fold_in(arg_keys[4], 71), 0),
        "in_inv": draw_in_inv(jax.random.fold_in(arg_keys[4], 71), 0),
    }


def reference(train_grads, query_grads, out_inv, in_inv):
    hi = lax.Precision.HIGHEST
    mid = jnp.einsum("qloi,lik->qlok", query_grads.astype(jnp.float32), in_inv, precision=hi)
    precond = jnp.einsum("loj,qljk->qlok", out_inv, mid, precision=hi).astype(jnp.bfloat16)
    flat_query = precond.reshape(QUERIES, -1)
    blocks = train_grads.reshape(TRAIN // ROW_DEV, ROW_DEV, -1)

    def score_block(block):
        return lax.dot_general(block, flat_query, (((1,), (1,)), ((), ())), preferred_element_type=jnp.float32)

    return lax.map(score_block, blocks).reshape(TRAIN, QUERIES)
```

```python
import functools

import jax
import jax.numpy as jnp
from jax import lax
from jax.experimental import pallas as pl
from jax.experimental.pallas import tpu as pltpu
from jax.sharding import Mesh
from jax.sharding import PartitionSpec as P

NAMES = ("zh", "zl", "yl", "x", "yh", "c")
SIZES = (2, 4, 2, 4, 4, 2)
FEAT = ("yh", "c")
NEAR = {0: (1, 3), 1: (3, 1)}
MASKS = {0: (0, 1, 3, 2), 1: (0, 3, 1, 2)}


def device_index(zh, zl, yl, x, yh, c):
    index = 0
    for size, at in zip(SIZES, (zh, zl, yl, x, yh, c)):
        index = index * size + at
    return index


def step_pairs(axis, step):
    pairs = []
    for z in range(8):
        for yl in range(2):
            for x in range(4):
                for yh in range(4):
                    for c in range(2):
                        mask = NEAR[c][step]
                        z2, x2 = z, x
                        if axis == "x":
                            x2 = x ^ mask
                        elif mask == 1:
                            z2 = z ^ 1
                        else:
                            z2 = (z + (1 if z % 2 else -1)) % 8
                        pairs.append(
                            (
                                device_index(z // 4, z % 4, yl, x, yh, c),
                                device_index(z2 // 4, z2 % 4, yl, x2, yh, c),
                            )
                        )
    return pairs


def exchange(block, axis, step):
    return lax.ppermute(block, NAMES, step_pairs(axis, step))


def precond_kernel(q_ref, out_inv_ref, in_inv_ref, send_ref):
    for layer in range(2):
        whole = q_ref[:, layer].astype(jnp.float32).reshape(128, 128)
        mid = jnp.dot(
            whole, in_inv_ref[layer], precision=lax.Precision.HIGHEST, preferred_element_type=jnp.float32
        )
        mixed = jnp.dot(
            out_inv_ref[layer], mid, precision=lax.Precision.HIGHEST, preferred_element_type=jnp.float32
        )
        mixed = mixed.astype(jnp.bfloat16).reshape(8, 16, 128)
        for copy in range(send_ref.shape[0]):
            send_ref[copy, :, layer] = mixed


def precondition(raw, out_inv, in_inv):
    return pl.pallas_call(
        precond_kernel,
        out_shape=jax.ShapeDtypeStruct((4, 8, 2, 16, 128), jnp.bfloat16),
        cost_estimate=pl.CostEstimate(flops=200_000_000, bytes_accessed=700_000, transcendentals=0),
    )(raw, out_inv, in_inv)


def nt_dot(a, b):
    return lax.dot_general(a, b, (((1,), (1,)), ((), ())), preferred_element_type=jnp.float32)


def early_kernel(pre_a_ref, pre_b_ref, train_ref, out_ref):
    out_ref[:128] = nt_dot(pre_a_ref[...], train_ref[...]).astype(jnp.bfloat16)
    out_ref[128:] = nt_dot(pre_b_ref[...], train_ref[...]).astype(jnp.bfloat16)


def late_kernel(place_ref, early_ref, pre_a_ref, pre_b_ref, train_ref, send_ref):
    for half, pre_ref in ((0, pre_a_ref), (1, pre_b_ref)):
        scores = nt_dot(pre_ref[...], train_ref[...]).astype(jnp.bfloat16)
        for block in range(8):
            send_ref[place_ref[half * 16 + block]] = early_ref[pl.ds(half * 128 + block * 16, 16)]
            send_ref[place_ref[half * 16 + 8 + block]] = scores[block * 16 : block * 16 + 16]


def early_scores(pre_a, pre_b, train):
    return pl.pallas_call(
        early_kernel,
        out_shape=jax.ShapeDtypeStruct((256, 512), jnp.bfloat16),
        cost_estimate=pl.CostEstimate(flops=1_073_741_824, bytes_accessed=7_000_000, transcendentals=0),
        compiler_params=pltpu.CompilerParams(vmem_limit_bytes=32 * 1024 * 1024),
    )(pre_a, pre_b, train)


def late_scores(place, early, pre_a, pre_b, train):
    whole = pl.BlockSpec(memory_space=pltpu.VMEM)
    return pl.pallas_call(
        late_kernel,
        out_shape=jax.ShapeDtypeStruct((32, 16, 512), jnp.bfloat16),
        in_specs=[pl.BlockSpec(memory_space=pltpu.SMEM)] + [whole] * 4,
        out_specs=whole,
        cost_estimate=pl.CostEstimate(flops=1_073_741_824, bytes_accessed=7_000_000, transcendentals=0),
        compiler_params=pltpu.CompilerParams(vmem_limit_bytes=32 * 1024 * 1024),
    )(place, early, pre_a, pre_b, train)


def body(train_grads, query_grads, out_inv, in_inv):
    raw = lax.all_to_all(query_grads, FEAT, 0, 0, tiled=True)
    send = precondition(raw, out_inv, in_inv)
    held = lax.all_to_all(send.reshape(32, 32, 128), ("zh", "yl", "yh", "c"), 0, 0, tiled=True)
    held = held.reshape(32, 4096)
    train = train_grads.reshape(512, 4096)
    a, b = held[:16], held[16:]
    for axes in (("x", "zl"), ("zl", "x")):
        pass
    for step in range(2):
        got_a, got_b = exchange(a, "x", step), exchange(b, "zl", step)
        a, b = jnp.concatenate([a, got_a]), jnp.concatenate([b, got_b])
    got_a, got_b = exchange(a, "zl", 0), exchange(b, "x", 0)
    a, b = jnp.concatenate([a, got_a]), jnp.concatenate([b, got_b])
    got_a, got_b = exchange(a, "zl", 1), exchange(b, "x", 1)
    early = early_scores(a, b, train)

    core, x, zl = lax.axis_index("c"), lax.axis_index("x"), lax.axis_index("zl")
    masks = jnp.where(core == 0, jnp.array(MASKS[0], jnp.int32), jnp.array(MASKS[1], jnp.int32))
    x_of, z_of = x ^ masks, zl ^ masks
    place_a = (z_of[:, None] * 4 + x_of[None, :]).reshape(16)
    place_b = (16 + z_of[None, :] * 4 + x_of[:, None]).reshape(16)
    place = jnp.concatenate([place_a, place_b]).astype(jnp.int32)

    partial = late_scores(place, early, got_a, got_b, train)
    parts = lax.all_to_all(partial.reshape(8, 64, 512), FEAT, 0, 0, tiled=True)
    total = jnp.sum(parts.astype(jnp.float32), axis=0)
    total = total.reshape(4, 2, 8, 512).transpose(1, 0, 2, 3).reshape(64, 512)
    return total.T


def solution(mesh):
    fine = Mesh(mesh.devices.reshape(SIZES), NAMES)
    rows, feat = ("zh", "zl", "yl", "x"), FEAT
    placed = (P(rows, None, feat, None), P(rows, None, feat, None), P(), P())
    return jax.shard_map(
        body, mesh=fine, in_specs=placed, out_specs=P(rows, feat), check_vma=False
    )
```

```python
import jax
import jax.numpy as jnp
from jax import lax
from jax.experimental import pallas as pl
from jax.experimental.pallas import tpu as pltpu
from jax.sharding import Mesh
from jax.sharding import PartitionSpec as P

NAMES = ("zh", "zl", "yl", "x", "yh", "c")
SIZES = (2, 4, 2, 4, 4, 2)
WHOLE = pl.BlockSpec(memory_space=pltpu.VMEM)
BIG = pltpu.CompilerParams(vmem_limit_bytes=24 * 1024 * 1024)
SMALL = pltpu.CompilerParams(vmem_limit_bytes=12 * 1024 * 1024)


def near(core):
    return (1, 3) if core == 0 else (3, 1)


def device_index(zh, zl, yl, x, yh, c):
    index = 0
    for size, at in zip(SIZES, (zh, zl, yl, x, yh, c)):
        index = index * size + at
    return index


def step_pairs(step, along_x, along_z):
    pairs = []
    for z in range(8):
        for yl in range(2):
            for x in range(4):
                for yh in range(4):
                    for c in range(2):
                        mask = near(c)[step]
                        z2, x2 = z, x
                        if along_x:
                            x2 = x ^ mask
                        if along_z:
                            z2 = z ^ 1 if mask == 1 else (z + (1 if z % 2 else -1)) % 8
                        pairs.append(
                            (
                                device_index(z // 4, z % 4, yl, x, yh, c),
                                device_index(z2 // 4, z2 % 4, yl, x2, yh, c),
                            )
                        )
    return pairs


def exchange(block, step, along_x, along_z):
    return lax.ppermute(block, NAMES, step_pairs(step, along_x, along_z))


def three_parts(value):
    top = value.astype(jnp.bfloat16)
    rest = value - top.astype(jnp.float32)
    middle = rest.astype(jnp.bfloat16)
    low = (rest - middle.astype(jnp.float32)).astype(jnp.bfloat16)
    return jnp.concatenate([top, middle, low])


def precond_kernel(raw_ref, out_inv_ref, in_inv_ref, pre_ref):
    feat = lax.axis_index("yh") * 2 + lax.axis_index("c")
    for layer in range(2):
        own = three_parts(out_inv_ref[layer, pl.ds(feat * 16, 16), :])
        mixed = []
        for q in range(8):
            whole = jnp.concatenate([raw_ref[f % 2, f // 2, q, layer] for f in range(8)])
            parts = jnp.dot(own, whole, preferred_element_type=jnp.float32)
            mixed.append((parts[32:] + parts[16:32]) + parts[:16])
        rows = jnp.dot(
            jnp.concatenate(mixed),
            in_inv_ref[layer],
            precision=lax.Precision.HIGHEST,
            preferred_element_type=jnp.float32,
        )
        rows = rows.astype(jnp.bfloat16).reshape(8, 16, 128)
        for copy in range(4):
            pre_ref[copy, :, layer] = rows


def precondition(raw, out_inv, in_inv):
    return pl.pallas_call(
        precond_kernel,
        out_shape=jax.ShapeDtypeStruct((4, 8, 2, 16, 128), jnp.bfloat16),
        in_specs=[WHOLE] * 3,
        out_specs=WHOLE,
        cost_estimate=pl.CostEstimate(flops=100_000_000, bytes_accessed=1_000_000, transcendentals=0),
        compiler_params=SMALL,
    )(raw, out_inv, in_inv)


def nt_dot(a, b):
    return lax.dot_general(a, b, (((1,), (1,)), ((), ())), preferred_element_type=jnp.float32)


def z_side(core):
    return (lax.axis_index("zl") & 1) ^ core


def split_rows(half, scores, keep_ref, send_ref):
    side = z_side(lax.axis_index("c"))
    mine = side if half == 0 else 1 - side
    for piece in range(2):
        keep_ref[piece * 64 : piece * 64 + 64] = scores[pl.ds(pl.multiple_of(piece * 128 + mine * 64, 64), 64), :]
        send_ref[piece * 64 : piece * 64 + 64] = scores[pl.ds(pl.multiple_of(piece * 128 + 64 - mine * 64, 64), 64), :]


def early_kernel(pre_0_ref, pre_1a_ref, pre_1b_ref, train_ref, keep_ref, send_ref, scores):
    pre = jnp.concatenate([pre_0_ref[...], pre_1a_ref[...], pre_1b_ref[...]])
    scores[...] = nt_dot(pre, train_ref[...])
    split_rows(0, scores, keep_ref, send_ref)


def middle_kernel(pre_a_ref, pre_b_ref, train_ref, scores_ref):
    scores_ref[...] = nt_dot(jnp.concatenate([pre_a_ref[...], pre_b_ref[...]]), train_ref[...])


def late_kernel(middle_ref, pre_a_ref, pre_b_ref, train_ref, keep_ref, send_ref, scores):
    scores[:128] = middle_ref[...]
    scores[128:] = nt_dot(jnp.concatenate([pre_a_ref[...], pre_b_ref[...]]), train_ref[...])
    split_rows(1, scores, keep_ref, send_ref)


def score_call(kernel, queries, *operands):
    half = jax.ShapeDtypeStruct((128, 512), jnp.float32)
    split = kernel is not middle_kernel
    return pl.pallas_call(
        kernel,
        out_shape=(half, half) if split else half,
        in_specs=[WHOLE] * len(operands),
        out_specs=(WHOLE, WHOLE) if split else WHOLE,
        scratch_shapes=[pltpu.VMEM((256, 512), jnp.float32)] if split else [],
        cost_estimate=pl.CostEstimate(
            flops=queries * 512 * 4096 * 2, bytes_accessed=queries * 8192 + 4_194_304, transcendentals=0
        ),
        compiler_params=BIG,
    )(*operands)


def block_places(half, core):
    x, zl = lax.axis_index("x"), lax.axis_index("zl")
    side = z_side(lax.axis_index("c"))
    first = jnp.where(core == 0, 1, 3)
    second = jnp.where(core == 0, 3, 1)
    mask_z = jnp.where(side == 0, 0 if half == 0 else 2, first if half == 0 else second)
    z1 = (zl ^ mask_z) >> 1
    places = []
    for of_piece in (0, second):
        for of_slot in (0, first):
            for zh in range(2):
                places.append((2 * zh + z1) * 4 + (x ^ of_piece ^ of_slot))
    return places


def combine_kernel(keep_0_ref, keep_1_ref, got_0_ref, got_1_ref, out_ref, total):
    core = lax.axis_index("c")
    for half, keep_ref in enumerate((keep_0_ref, keep_1_ref)):
        for block, place in enumerate(block_places(half, core)):
            total[place] = keep_ref[block * 16 : block * 16 + 16]
    for half, got_ref in enumerate((got_0_ref, got_1_ref)):
        for block, place in enumerate(block_places(half, 1 - core)):
            total[place] = total[place] + got_ref[1 - core, block * 16 : block * 16 + 16]
    out_ref[...] = total[...].astype(jnp.bfloat16)


def combine(keeps, gots):
    return pl.pallas_call(
        combine_kernel,
        out_shape=jax.ShapeDtypeStruct((16, 16, 512), jnp.bfloat16),
        in_specs=[WHOLE] * 4,
        out_specs=WHOLE,
        scratch_shapes=[pltpu.VMEM((16, 16, 512), jnp.float32)],
        cost_estimate=pl.CostEstimate(flops=262_144, bytes_accessed=2_000_000, transcendentals=0),
        compiler_params=SMALL,
    )(*keeps, *gots)


def sum_kernel(parts_ref, out_ref):
    for x in range(4):
        total = parts_ref[0, x].astype(jnp.float32)
        for chip in range(1, 4):
            total = total + parts_ref[chip, x].astype(jnp.float32)
        out_ref[x * 8 : x * 8 + 8] = total[:8]
        out_ref[32 + x * 8 : 40 + x * 8] = total[8:]


def final_sum(parts):
    return pl.pallas_call(
        sum_kernel,
        out_shape=jax.ShapeDtypeStruct((64, 512), jnp.float32),
        in_specs=[WHOLE],
        out_specs=WHOLE,
        cost_estimate=pl.CostEstimate(flops=131_072, bytes_accessed=400_000, transcendentals=0),
        compiler_params=SMALL,
    )(parts)


def body(train_grads, query_grads, out_inv, in_inv):
    copies = jnp.broadcast_to(query_grads[None], (4,) + query_grads.shape)
    raw = lax.all_gather(lax.all_to_all(copies, "yh", 0, 0, tiled=True), "c")
    pre = precondition(raw, out_inv, in_inv).reshape(4, 8, 32, 128)
    pre = lax.all_to_all(pre, ("zh", "yl"), 0, 0, tiled=True)
    held = pre.reshape(32, 4096)
    train = train_grads.reshape(512, 4096)
    along_x, along_z, along_both = (True, False), (False, True), (True, True)
    square = jnp.concatenate([held] + [exchange(held, 0, *way) for way in (along_x, along_z, along_both)])
    square, train = lax.optimization_barrier((square, train))
    first, second = square[:64], square[64:]
    x_first, z_second = exchange(first, 1, *along_x), exchange(second, 1, *along_z)
    x_second, z_first = exchange(second, 1, *along_x), exchange(first, 1, *along_z)
    both_first, both_second = exchange(x_first, 1, *along_z), exchange(z_second, 1, *along_x)

    keep_0, send_0 = score_call(early_kernel, 256, square, x_first, x_second, train)
    got_0 = lax.all_gather(send_0, "c")
    middle = score_call(middle_kernel, 128, z_first, z_second, train)
    keep_1, send_1 = score_call(late_kernel, 128, middle, both_first, both_second, train)
    got_1 = lax.all_gather(send_1, "c")
    chip_sum = combine((keep_0, keep_1), (got_0, got_1))
    parts = lax.all_to_all(chip_sum.reshape(4, 4, 16, 512), "yh", 0, 0, tiled=True)
    return final_sum(parts).T


def solution(mesh):
    fine = Mesh(mesh.devices.reshape(SIZES), NAMES)
    rows, feat = ("zh", "zl", "yl", "x"), ("yh", "c")
    placed = (P(rows, None, feat, None), P(rows, None, feat, None), P(), P())
    return jax.shard_map(
        body, mesh=fine, in_specs=placed, out_specs=P(rows, feat), check_vma=False
    )
```

```python
import itertools

import jax
import jax.numpy as jnp
from jax import lax
from jax.experimental import pallas as pl
from jax.experimental.pallas import tpu as pltpu
from jax.sharding import Mesh
from jax.sharding import PartitionSpec as P

NAMES = ("zh", "zl", "yl", "x", "yh", "c")
SIZES = (2, 4, 2, 4, 4, 2)
WHOLE = pl.BlockSpec(memory_space=pltpu.VMEM)
BIG = pltpu.CompilerParams(vmem_limit_bytes=24 * 1024 * 1024)
SMALL = pltpu.CompilerParams(vmem_limit_bytes=12 * 1024 * 1024)


def near(axis, core):
    return (1, 3) if (axis == "x") == (core == 0) else (3, 1)


def device_index(zh, zl, yl, x, yh, c):
    index = 0
    for size, at in zip(SIZES, (zh, zl, yl, x, yh, c)):
        index = index * size + at
    return index


def z_neighbour(z, mask):
    return z ^ 1 if mask == 1 else (z + (1 if z % 2 else -1)) % 8


def every_device():
    return itertools.product(range(8), range(2), range(4), range(4), range(2))


def square_groups():
    groups = {}
    for z, yl, x, yh, c in every_device():
        x_pair, z_pair = (x, x ^ near("x", c)[0]), (z, z_neighbour(z, near("z", c)[0]))
        by_parity = lambda pair: sorted(pair, key=lambda at: at % 2)
        corners = [(z2, x2) for z2 in by_parity(z_pair) for x2 in by_parity(x_pair)]
        groups[tuple(device_index(z2 // 4, z2 % 4, yl, x2, yh, c) for z2, x2 in corners)] = None
    return [list(group) for group in groups]


def step_pairs(along_x):
    pairs = []
    for z, yl, x, yh, c in every_device():
        z2, x2 = (z, x ^ near("x", c)[1]) if along_x else (z_neighbour(z, near("z", c)[1]), x)
        pairs.append((device_index(z // 4, z % 4, yl, x, yh, c), device_index(z2 // 4, z2 % 4, yl, x2, yh, c)))
    return pairs


def exchange(block, along_x):
    return lax.ppermute(block, NAMES, step_pairs(along_x))


def three_parts(value):
    top = value.astype(jnp.bfloat16)
    rest = value - top.astype(jnp.float32)
    middle = rest.astype(jnp.bfloat16)
    low = (rest - middle.astype(jnp.float32)).astype(jnp.bfloat16)
    return jnp.concatenate([top, middle, low])


def prepare_kernel(query_ref, out_inv_ref, in_inv_ref, copies_ref, own_ref, factor_ref, rows, sems):
    feat = lax.axis_index("yh") * 2 + lax.axis_index("c")
    moves = [pltpu.make_async_copy(query_ref, copies_ref.at[copy], sems.at[copy]) for copy in range(4)]
    own_rows = out_inv_ref.at[:, pl.ds(pl.multiple_of(feat * 16, 16), 16), :]
    moves.append(pltpu.make_async_copy(own_rows, rows, sems.at[4]))
    moves.append(pltpu.make_async_copy(in_inv_ref, factor_ref, sems.at[5]))
    for move in moves:
        move.start()
    moves[4].wait()
    for layer in range(2):
        own_ref[layer] = three_parts(rows[layer])
    for move in moves[:4] + moves[5:]:
        move.wait()


def prepare(queries, out_inv, in_inv):
    far = pl.BlockSpec(memory_space=pltpu.HBM)
    return pl.pallas_call(
        prepare_kernel,
        out_shape=(
            jax.ShapeDtypeStruct((4,) + queries.shape, jnp.bfloat16),
            jax.ShapeDtypeStruct((2, 48, 128), jnp.bfloat16),
            jax.ShapeDtypeStruct((2, 128, 128), jnp.float32),
        ),
        in_specs=[far] * 3,
        out_specs=(WHOLE,) * 3,
        scratch_shapes=[pltpu.VMEM((2, 16, 128), jnp.float32), pltpu.SemaphoreType.DMA((6,))],
        cost_estimate=pl.CostEstimate(flops=10_000, bytes_accessed=700_000, transcendentals=0),
        compiler_params=SMALL,
    )(*(pltpu.with_memory_space_constraint(each, pltpu.HBM) for each in (queries, out_inv, in_inv)))


def precond_kernel(raw_ref, own_ref, in_inv_ref, pre_ref):
    for layer in range(2):
        mixed = []
        for q in range(8):
            whole = jnp.concatenate([raw_ref[f % 2, f // 2, q, layer] for f in range(8)])
            parts = jnp.dot(own_ref[layer], whole, preferred_element_type=jnp.float32)
            mixed.append((parts[32:] + parts[16:32]) + parts[:16])
        rows = jnp.dot(
            jnp.concatenate(mixed),
            in_inv_ref[layer],
            precision=lax.Precision.HIGHEST,
            preferred_element_type=jnp.float32,
        )
        pre_ref[:, layer] = rows.astype(jnp.bfloat16).reshape(8, 16, 128)


def precondition(raw, own, in_inv):
    return pl.pallas_call(
        precond_kernel,
        out_shape=jax.ShapeDtypeStruct((8, 2, 16, 128), jnp.bfloat16),
        in_specs=[WHOLE] * 3,
        out_specs=WHOLE,
        cost_estimate=pl.CostEstimate(flops=100_000_000, bytes_accessed=1_000_000, transcendentals=0),
        compiler_params=SMALL,
    )(raw, own, in_inv)


def flatten_kernel(train_ref, flat_ref, held, sems):
    parts = 4
    rows = held.shape[0] // parts
    moves = []
    for part in range(parts):
        window = pl.ds(part * rows, rows)
        moves.append(pltpu.make_async_copy(train_ref.at[window], held.at[window], sems.at[part]))
        moves[part].start()
    for part in range(parts):
        moves[part].wait()
        window = pl.ds(part * rows, rows)
        flat_ref[window, :] = held[window].reshape(rows, 4096)


def flatten(train):
    return pl.pallas_call(
        flatten_kernel,
        out_shape=jax.ShapeDtypeStruct((512, 4096), jnp.bfloat16),
        in_specs=[pl.BlockSpec(memory_space=pltpu.HBM)],
        out_specs=WHOLE,
        scratch_shapes=[pltpu.VMEM((512, 32, 128), jnp.bfloat16), pltpu.SemaphoreType.DMA((4,))],
        cost_estimate=pl.CostEstimate(flops=0, bytes_accessed=8_388_608, transcendentals=0),
        compiler_params=BIG,
    )(pltpu.with_memory_space_constraint(train, pltpu.HBM))


def nt_dot(a, b):
    return lax.dot_general(a, b, (((1,), (1,)), ((), ())), preferred_element_type=jnp.float32)


def split_rows(pieces, keep_ref, send_ref):
    core = lax.axis_index("c")
    for index, (piece, base) in enumerate(pieces):
        rows = slice(index * 64, index * 64 + 64)
        keep_ref[rows] = piece[pl.ds(pl.multiple_of(base + core * 64, 64), 64), :]
        send_ref[rows] = piece[pl.ds(pl.multiple_of(base + 64 - core * 64, 64), 64), :]


def score_kernel(*refs):
    *pieces, train_ref, keep_ref, send_ref, scores = refs
    scores[...] = nt_dot(jnp.concatenate([piece[...] for piece in pieces]), train_ref[...])
    split_rows(((scores, 0), (scores, 128)), keep_ref, send_ref)


def half_scores(pieces, train):
    half = jax.ShapeDtypeStruct((128, 512), jnp.float32)
    return pl.pallas_call(
        score_kernel,
        out_shape=(half, half),
        in_specs=[WHOLE] * (len(pieces) + 1),
        out_specs=(WHOLE, WHOLE),
        scratch_shapes=[pltpu.VMEM((256, 512), jnp.float32)],
        cost_estimate=pl.CostEstimate(flops=1_073_741_824, bytes_accessed=6_291_456, transcendentals=0),
        compiler_params=BIG,
    )(*pieces, train)


def block_places(half, core):
    x_first, x_second = [jnp.where(core == 0, near("x", 0)[step], near("x", 1)[step]) for step in range(2)]
    z_first, z_second = [jnp.where(core == 0, near("z", 0)[step], near("z", 1)[step]) for step in range(2)]
    x = lax.axis_index("x")
    z = lax.axis_index("zl") ^ (z_second if half else 0)
    z1 = jnp.where((z & 1) == lax.axis_index("c"), z, z ^ z_first) >> 1
    places = []
    for x_base in (x, x ^ x_second):
        for parity in range(2):
            x_of = jnp.where((x_base & 1) == parity, x_base, x_base ^ x_first)
            places += [(2 * zh + z1) * 4 + x_of for zh in range(2)]
    return places


def combine_kernel(keep_0_ref, keep_1_ref, got_0_ref, got_1_ref, out_ref, total):
    core = lax.axis_index("c")
    for half, keep_ref in enumerate((keep_0_ref, keep_1_ref)):
        for block, place in enumerate(block_places(half, core)):
            total[place] = keep_ref[block * 16 : block * 16 + 16]
    for half, got_ref in enumerate((got_0_ref, got_1_ref)):
        for block, place in enumerate(block_places(half, 1 - core)):
            total[place] = total[place] + got_ref[1 - core, block * 16 : block * 16 + 16]
    out_ref[...] = total[...].astype(jnp.bfloat16)


def combine(keeps, gots):
    return pl.pallas_call(
        combine_kernel,
        out_shape=jax.ShapeDtypeStruct((16, 16, 512), jnp.bfloat16),
        in_specs=[WHOLE] * 4,
        out_specs=WHOLE,
        scratch_shapes=[pltpu.VMEM((16, 16, 512), jnp.float32)],
        cost_estimate=pl.CostEstimate(flops=262_144, bytes_accessed=2_000_000, transcendentals=0),
        compiler_params=SMALL,
    )(*keeps, *gots)


def sum_kernel(parts_ref, out_ref):
    for x in range(4):
        total = parts_ref[0, x].astype(jnp.float32)
        for chip in range(1, 4):
            total = total + parts_ref[chip, x].astype(jnp.float32)
        out_ref[x * 8 : x * 8 + 8] = total[:8]
        out_ref[32 + x * 8 : 40 + x * 8] = total[8:]


def final_sum(parts):
    return pl.pallas_call(
        sum_kernel,
        out_shape=jax.ShapeDtypeStruct((64, 512), jnp.float32),
        in_specs=[WHOLE],
        out_specs=WHOLE,
        cost_estimate=pl.CostEstimate(flops=131_072, bytes_accessed=400_000, transcendentals=0),
        compiler_params=SMALL,
    )(parts)


def body(train_grads, query_grads, out_inv, in_inv):
    copies, own, factor = prepare(query_grads, out_inv, in_inv)
    raw = lax.all_gather(lax.all_to_all(copies, "yh", 0, 0, tiled=True), "c")
    pre = precondition(raw, own, factor).reshape(8, 32, 128)
    pre = lax.all_gather(lax.all_gather(pre, "zh"), "yl", axis=1)
    held = pre.reshape(32, 4096)
    train = flatten(train_grads.reshape(512, 32, 128))
    square = lax.all_to_all(
        jnp.broadcast_to(held[None], (4,) + held.shape), NAMES, 0, 0, tiled=True, axis_index_groups=square_groups()
    ).reshape(128, 4096)
    first, second = square[:64], square[64:]
    x_first, z_second = exchange(first, True), exchange(second, False)
    x_second, z_first = exchange(second, True), exchange(first, False)
    both_first, both_second = exchange(x_first, False), exchange(z_second, True)

    keep_0, send_0 = half_scores((square, x_first, x_second), train)
    got_0 = lax.all_gather(send_0, "c")
    keep_1, send_1 = half_scores((z_first, z_second, both_first, both_second), train)
    got_1 = lax.all_gather(send_1, "c")
    chip_sum = combine((keep_0, keep_1), (got_0, got_1))
    parts = lax.all_to_all(chip_sum.reshape(4, 4, 16, 512), "yh", 0, 0, tiled=True)
    return final_sum(parts).T


def solution(mesh):
    fine = Mesh(mesh.devices.reshape(SIZES), NAMES)
    rows, feat = ("zh", "zl", "yl", "x"), ("yh", "c")
    placed = (P(rows, None, feat, None), P(rows, None, feat, None), P(), P())
    return jax.shard_map(
        body, mesh=fine, in_specs=placed, out_specs=P(rows, feat), check_vma=False
    )
```

```python
import itertools

import jax
import jax.numpy as jnp
from jax import lax
from jax.experimental import pallas as pl
from jax.experimental.pallas import tpu as pltpu
from jax.sharding import Mesh
from jax.sharding import PartitionSpec as P

NAMES = ("zh", "zl", "yl", "x", "yh", "c")
SIZES = (2, 4, 2, 4, 4, 2)
WHOLE = pl.BlockSpec(memory_space=pltpu.VMEM)
BIG = pltpu.CompilerParams(vmem_limit_bytes=24 * 1024 * 1024)
SMALL = pltpu.CompilerParams(vmem_limit_bytes=12 * 1024 * 1024)


def near(axis, core):
    return (1, 3) if (axis == "x") == (core == 0) else (3, 1)


def device_index(zh, zl, yl, x, yh, c):
    index = 0
    for size, at in zip(SIZES, (zh, zl, yl, x, yh, c)):
        index = index * size + at
    return index


def z_neighbour(z, mask):
    return z ^ 1 if mask == 1 else (z + (1 if z % 2 else -1)) % 8


def every_device():
    return itertools.product(range(8), range(2), range(4), range(4), range(2))


def square_groups():
    groups = {}
    for z, yl, x, yh, c in every_device():
        x_pair, z_pair = (x, x ^ near("x", c)[0]), (z, z_neighbour(z, near("z", c)[0]))
        by_parity = lambda pair: sorted(pair, key=lambda at: at % 2)
        corners = [(z2, x2) for z2 in by_parity(z_pair) for x2 in by_parity(x_pair)]
        groups[tuple(device_index(z2 // 4, z2 % 4, yl, x2, yh, c) for z2, x2 in corners)] = None
    return [list(group) for group in groups]


def step_pairs(along_x):
    pairs = []
    for z, yl, x, yh, c in every_device():
        z2, x2 = (z, x ^ near("x", c)[1]) if along_x else (z_neighbour(z, near("z", c)[1]), x)
        pairs.append((device_index(z // 4, z % 4, yl, x, yh, c), device_index(z2 // 4, z2 % 4, yl, x2, yh, c)))
    return pairs


def exchange(block, along_x):
    return lax.ppermute(block, NAMES, step_pairs(along_x))


def three_parts(value):
    top = value.astype(jnp.bfloat16)
    rest = value - top.astype(jnp.float32)
    middle = rest.astype(jnp.bfloat16)
    low = (rest - middle.astype(jnp.float32)).astype(jnp.bfloat16)
    return jnp.concatenate([top, middle, low])


def prepare_kernel(query_ref, out_inv_ref, in_inv_ref, copies_ref, own_ref, factor_ref, sems):
    feat = lax.axis_index("yh") * 2 + lax.axis_index("c")
    moves = [pltpu.make_async_copy(query_ref, copies_ref.at[copy], sems.at[copy]) for copy in range(4)]
    own_rows = out_inv_ref.at[:, pl.ds(pl.multiple_of(feat * 16, 16), 16), :]
    moves.append(pltpu.make_async_copy(own_rows, own_ref, sems.at[4]))
    moves.append(pltpu.make_async_copy(in_inv_ref, factor_ref, sems.at[5]))
    for move in moves:
        move.start()
    for move in moves:
        move.wait()


def prepare(queries, out_inv, in_inv):
    far = pl.BlockSpec(memory_space=pltpu.HBM)
    return pl.pallas_call(
        prepare_kernel,
        out_shape=(
            jax.ShapeDtypeStruct((4,) + queries.shape, jnp.bfloat16),
            jax.ShapeDtypeStruct((2, 16, 128), jnp.float32),
            jax.ShapeDtypeStruct((2, 128, 128), jnp.float32),
        ),
        in_specs=[far] * 3,
        out_specs=(WHOLE,) * 3,
        scratch_shapes=[pltpu.SemaphoreType.DMA((6,))],
        cost_estimate=pl.CostEstimate(flops=0, bytes_accessed=700_000, transcendentals=0),
        compiler_params=SMALL,
    )(*(pltpu.with_memory_space_constraint(each, pltpu.HBM) for each in (queries, out_inv, in_inv)))


def precond_kernel(raw_ref, own_ref, in_inv_ref, pre_ref):
    for layer in range(2):
        own = three_parts(own_ref[layer])
        mixed = []
        for q in range(8):
            whole = jnp.concatenate([raw_ref[f % 2, f // 2, q, layer] for f in range(8)])
            parts = jnp.dot(own, whole, preferred_element_type=jnp.float32)
            mixed.append((parts[32:] + parts[16:32]) + parts[:16])
        rows = jnp.dot(
            jnp.concatenate(mixed),
            in_inv_ref[layer],
            precision=lax.Precision.HIGHEST,
            preferred_element_type=jnp.float32,
        )
        pre_ref[:, layer] = rows.astype(jnp.bfloat16).reshape(8, 16, 128)


def precondition(raw, own, in_inv):
    return pl.pallas_call(
        precond_kernel,
        out_shape=jax.ShapeDtypeStruct((8, 2, 16, 128), jnp.bfloat16),
        in_specs=[WHOLE] * 3,
        out_specs=WHOLE,
        cost_estimate=pl.CostEstimate(flops=100_000_000, bytes_accessed=1_000_000, transcendentals=0),
        compiler_params=SMALL,
    )(raw, own, in_inv)


def flatten_kernel(train_ref, flat_ref, held, sems):
    parts = 8
    rows = held.shape[0] // parts
    moves = []
    for part in range(parts):
        window = pl.ds(part * rows, rows)
        moves.append(pltpu.make_async_copy(train_ref.at[window], held.at[window], sems.at[part]))
        moves[part].start()
    for part in range(parts):
        moves[part].wait()
        window = pl.ds(part * rows, rows)
        flat_ref[window, :] = held[window].reshape(rows, 4096)


def flatten(train):
    return pl.pallas_call(
        flatten_kernel,
        out_shape=jax.ShapeDtypeStruct((512, 4096), jnp.bfloat16),
        in_specs=[pl.BlockSpec(memory_space=pltpu.HBM)],
        out_specs=WHOLE,
        scratch_shapes=[pltpu.VMEM((512, 32, 128), jnp.bfloat16), pltpu.SemaphoreType.DMA((8,))],
        cost_estimate=pl.CostEstimate(flops=0, bytes_accessed=8_388_608, transcendentals=0),
        compiler_params=BIG,
    )(pltpu.with_memory_space_constraint(train, pltpu.HBM))


def nt_dot(a, b):
    return lax.dot_general(a, b, (((1,), (1,)), ((), ())), preferred_element_type=jnp.float32)


def split_rows(pieces, keep_ref, send_ref):
    core = lax.axis_index("c")
    for index, (piece, base) in enumerate(pieces):
        rows = slice(index * 64, index * 64 + 64)
        keep_ref[rows] = piece[pl.ds(pl.multiple_of(base + core * 64, 64), 64), :]
        send_ref[rows] = piece[pl.ds(pl.multiple_of(base + 64 - core * 64, 64), 64), :]


def score_kernel(*refs):
    *pieces, train_ref, keep_ref, send_ref, scores = refs
    scores[...] = nt_dot(jnp.concatenate([piece[...] for piece in pieces]), train_ref[...])
    split_rows(((scores, 0), (scores, 128)), keep_ref, send_ref)


def half_scores(pieces, train):
    half = jax.ShapeDtypeStruct((128, 512), jnp.float32)
    return pl.pallas_call(
        score_kernel,
        out_shape=(half, half),
        in_specs=[WHOLE] * (len(pieces) + 1),
        out_specs=(WHOLE, WHOLE),
        scratch_shapes=[pltpu.VMEM((256, 512), jnp.float32)],
        cost_estimate=pl.CostEstimate(flops=1_073_741_824, bytes_accessed=6_291_456, transcendentals=0),
        compiler_params=BIG,
    )(*pieces, train)


def block_places(half, core):
    x_first, x_second = [jnp.where(core == 0, near("x", 0)[step], near("x", 1)[step]) for step in range(2)]
    z_first, z_second = [jnp.where(core == 0, near("z", 0)[step], near("z", 1)[step]) for step in range(2)]
    x = lax.axis_index("x")
    z = lax.axis_index("zl") ^ (z_second if half else 0)
    z1 = jnp.where((z & 1) == lax.axis_index("c"), z, z ^ z_first) >> 1
    places = []
    for x_base in (x, x ^ x_second):
        for parity in range(2):
            x_of = jnp.where((x_base & 1) == parity, x_base, x_base ^ x_first)
            places += [(2 * zh + z1) * 4 + x_of for zh in range(2)]
    return places


def combine_kernel(keep_0_ref, keep_1_ref, got_0_ref, got_1_ref, out_ref, own_ref, total):
    core = lax.axis_index("c")
    for half, keep_ref in enumerate((keep_0_ref, keep_1_ref)):
        for block, place in enumerate(block_places(half, core)):
            total[place] = keep_ref[block * 16 : block * 16 + 16]
    for half, got_ref in enumerate((got_0_ref, got_1_ref)):
        for block, place in enumerate(block_places(half, 1 - core)):
            total[place] = total[place] + got_ref[1 - core, block * 16 : block * 16 + 16]
    out_ref[...] = total[...].astype(jnp.bfloat16)
    own_ref[...] = total[pl.ds(lax.axis_index("yh") * 4, 4)]


def combine(keeps, gots):
    return pl.pallas_call(
        combine_kernel,
        out_shape=(
            jax.ShapeDtypeStruct((16, 16, 512), jnp.bfloat16),
            jax.ShapeDtypeStruct((4, 16, 512), jnp.float32),
        ),
        in_specs=[WHOLE] * 4,
        out_specs=(WHOLE, WHOLE),
        scratch_shapes=[pltpu.VMEM((16, 16, 512), jnp.float32)],
        cost_estimate=pl.CostEstimate(flops=262_144, bytes_accessed=2_000_000, transcendentals=0),
        compiler_params=SMALL,
    )(*keeps, *gots)


def sum_kernel(parts_ref, own_ref, out_ref):
    chip = lax.axis_index("yh")
    for x in range(4):
        total = own_ref[x]
        for step in range(1, 4):
            total = total + parts_ref[(chip + step) & 3, x].astype(jnp.float32)
        out_ref[x * 8 : x * 8 + 8] = total[:8]
        out_ref[32 + x * 8 : 40 + x * 8] = total[8:]


def final_sum(parts, own):
    return pl.pallas_call(
        sum_kernel,
        out_shape=jax.ShapeDtypeStruct((64, 512), jnp.float32),
        in_specs=[WHOLE] * 2,
        out_specs=WHOLE,
        cost_estimate=pl.CostEstimate(flops=131_072, bytes_accessed=500_000, transcendentals=0),
        compiler_params=SMALL,
    )(parts, own)


def body(train_grads, query_grads, out_inv, in_inv):
    copies, own, factor = prepare(query_grads, out_inv, in_inv)
    raw = lax.all_gather(lax.all_to_all(copies, "yh", 0, 0, tiled=True), "c")
    pre = precondition(raw, own, factor).reshape(8, 32, 128)
    pre = lax.all_gather(lax.all_gather(pre, "zh"), "yl", axis=1)
    held = pre.reshape(32, 4096)
    train = flatten(train_grads.reshape(512, 32, 128))
    square = lax.all_to_all(
        jnp.broadcast_to(held[None], (4,) + held.shape), NAMES, 0, 0, tiled=True, axis_index_groups=square_groups()
    ).reshape(128, 4096)
    first, second = square[:64], square[64:]
    x_first, z_second = exchange(first, True), exchange(second, False)
    x_second, z_first = exchange(second, True), exchange(first, False)
    both_first, both_second = exchange(x_first, False), exchange(z_second, True)

    keep_0, send_0 = half_scores((square, x_first, x_second), train)
    got_0 = lax.all_gather(send_0, "c")
    keep_1, send_1 = half_scores((z_first, z_second, both_first, both_second), train)
    got_1 = lax.all_gather(send_1, "c")
    chip_sum, own_sum = combine((keep_0, keep_1), (got_0, got_1))
    parts = lax.all_to_all(chip_sum.reshape(4, 4, 16, 512), "yh", 0, 0, tiled=True)
    return final_sum(parts, own_sum).T


def solution(mesh):
    fine = Mesh(mesh.devices.reshape(SIZES), NAMES)
    rows, feat = ("zh", "zl", "yl", "x"), ("yh", "c")
    placed = (P(rows, None, feat, None), P(rows, None, feat, None), P(), P())
    return jax.shard_map(
        body, mesh=fine, in_specs=placed, out_specs=P(rows, feat), check_vma=False
    )
```

```python
import itertools

import jax
import jax.numpy as jnp
from jax import lax
from jax.experimental import pallas as pl
from jax.experimental.pallas import tpu as pltpu
from jax.sharding import Mesh
from jax.sharding import PartitionSpec as P

NAMES = ("zh", "zl", "yl", "x", "yh", "c")
SIZES = (2, 4, 2, 4, 4, 2)
WHOLE = pl.BlockSpec(memory_space=pltpu.VMEM)
BIG = pltpu.CompilerParams(vmem_limit_bytes=24 * 1024 * 1024)
SMALL = pltpu.CompilerParams(vmem_limit_bytes=12 * 1024 * 1024)


def near(axis, core):
    return (1, 3) if (axis == "x") == (core == 0) else (3, 1)


def device_index(zh, zl, yl, x, yh, c):
    index = 0
    for size, at in zip(SIZES, (zh, zl, yl, x, yh, c)):
        index = index * size + at
    return index


def z_neighbour(z, mask):
    return z ^ 1 if mask == 1 else (z + (1 if z % 2 else -1)) % 8


def every_device():
    return itertools.product(range(8), range(2), range(4), range(4), range(2))


def square_groups():
    groups = {}
    for z, yl, x, yh, c in every_device():
        x_pair, z_pair = (x, x ^ near("x", c)[0]), (z, z_neighbour(z, near("z", c)[0]))
        by_parity = lambda pair: sorted(pair, key=lambda at: at % 2)
        corners = [(z2, x2) for z2 in by_parity(z_pair) for x2 in by_parity(x_pair)]
        groups[tuple(device_index(z2 // 4, z2 % 4, y2, x2, yh, c) for z2, x2 in corners for y2 in range(2))] = None
    return [list(group) for group in groups]


def step_pairs(along_x):
    pairs = []
    for z, yl, x, yh, c in every_device():
        z2, x2 = (z, x ^ near("x", c)[1]) if along_x else (z_neighbour(z, near("z", c)[1]), x)
        pairs.append((device_index(z // 4, z % 4, yl, x, yh, c), device_index(z2 // 4, z2 % 4, yl, x2, yh, c)))
    return pairs


def exchange(block, along_x):
    return lax.ppermute(block, NAMES, step_pairs(along_x))


def three_parts(value):
    top = value.astype(jnp.bfloat16)
    rest = value - top.astype(jnp.float32)
    middle = rest.astype(jnp.bfloat16)
    low = (rest - middle.astype(jnp.float32)).astype(jnp.bfloat16)
    return jnp.concatenate([top, middle, low])


def prepare_kernel(query_ref, out_inv_ref, in_inv_ref, copies_ref, own_ref, factor_ref, sems):
    feat = lax.axis_index("yh") * 2 + lax.axis_index("c")
    moves = [pltpu.make_async_copy(query_ref, copies_ref.at[copy], sems.at[copy]) for copy in range(4)]
    own_rows = out_inv_ref.at[:, pl.ds(pl.multiple_of(feat * 16, 16), 16), :]
    moves.append(pltpu.make_async_copy(own_rows, own_ref, sems.at[4]))
    moves.append(pltpu.make_async_copy(in_inv_ref, factor_ref, sems.at[5]))
    for move in moves:
        move.start()
    for move in moves:
        move.wait()


def prepare(queries, out_inv, in_inv):
    far = pl.BlockSpec(memory_space=pltpu.HBM)
    return pl.pallas_call(
        prepare_kernel,
        out_shape=(
            jax.ShapeDtypeStruct((4,) + queries.shape, jnp.bfloat16),
            jax.ShapeDtypeStruct((2, 16, 128), jnp.float32),
            jax.ShapeDtypeStruct((2, 128, 128), jnp.float32),
        ),
        in_specs=[far] * 3,
        out_specs=(WHOLE,) * 3,
        scratch_shapes=[pltpu.SemaphoreType.DMA((6,))],
        cost_estimate=pl.CostEstimate(flops=0, bytes_accessed=700_000, transcendentals=0),
        compiler_params=SMALL,
    )(*(pltpu.with_memory_space_constraint(each, pltpu.HBM) for each in (queries, out_inv, in_inv)))


def precond_kernel(raw_ref, own_ref, in_inv_ref, pre_ref):
    for layer in range(2):
        own = three_parts(own_ref[layer])
        mixed = []
        for q in range(8):
            whole = jnp.concatenate([raw_ref[f % 2, f // 2, q, layer] for f in range(8)])
            parts = jnp.dot(own, whole, preferred_element_type=jnp.float32)
            mixed.append((parts[32:] + parts[16:32]) + parts[:16])
        rows = jnp.dot(
            jnp.concatenate(mixed),
            in_inv_ref[layer],
            precision=lax.Precision.HIGHEST,
            preferred_element_type=jnp.float32,
        )
        pre_ref[:, layer] = rows.astype(jnp.bfloat16).reshape(8, 16, 128)


def precondition(raw, own, in_inv):
    return pl.pallas_call(
        precond_kernel,
        out_shape=jax.ShapeDtypeStruct((8, 2, 16, 128), jnp.bfloat16),
        in_specs=[WHOLE] * 3,
        out_specs=WHOLE,
        cost_estimate=pl.CostEstimate(flops=100_000_000, bytes_accessed=1_000_000, transcendentals=0),
        compiler_params=SMALL,
    )(raw, own, in_inv)


def flatten_kernel(train_ref, flat_ref, held, sems):
    parts = 8
    rows = held.shape[0] // parts
    moves = []
    for part in range(parts):
        window = pl.ds(part * rows, rows)
        moves.append(pltpu.make_async_copy(train_ref.at[window], held.at[window], sems.at[part]))
        moves[part].start()
    for part in range(parts):
        moves[part].wait()
        window = pl.ds(part * rows, rows)
        flat_ref[window, :] = held[window].reshape(rows, 4096)


def flatten(train):
    return pl.pallas_call(
        flatten_kernel,
        out_shape=jax.ShapeDtypeStruct((512, 4096), jnp.bfloat16),
        in_specs=[pl.BlockSpec(memory_space=pltpu.HBM)],
        out_specs=WHOLE,
        scratch_shapes=[pltpu.VMEM((512, 32, 128), jnp.bfloat16), pltpu.SemaphoreType.DMA((8,))],
        cost_estimate=pl.CostEstimate(flops=0, bytes_accessed=8_388_608, transcendentals=0),
        compiler_params=BIG,
    )(pltpu.with_memory_space_constraint(train, pltpu.HBM))


def nt_dot(a, b):
    return lax.dot_general(a, b, (((1,), (1,)), ((), ())), preferred_element_type=jnp.float32)


def split_rows(pieces, keep_ref, send_ref):
    core = lax.axis_index("c")
    for index, (piece, base) in enumerate(pieces):
        rows = slice(index * 64, index * 64 + 64)
        keep_ref[rows] = piece[pl.ds(pl.multiple_of(base + core * 64, 64), 64), :]
        send_ref[rows] = piece[pl.ds(pl.multiple_of(base + 64 - core * 64, 64), 64), :]


def score_kernel(*refs):
    *pieces, train_ref, keep_ref, send_ref, scores = refs
    scores[...] = nt_dot(jnp.concatenate([piece[...] for piece in pieces]), train_ref[...])
    split_rows(((scores, 0), (scores, 128)), keep_ref, send_ref)


def half_scores(pieces, train):
    half = jax.ShapeDtypeStruct((128, 512), jnp.float32)
    return pl.pallas_call(
        score_kernel,
        out_shape=(half, half),
        in_specs=[WHOLE] * (len(pieces) + 1),
        out_specs=(WHOLE, WHOLE),
        scratch_shapes=[pltpu.VMEM((256, 512), jnp.float32)],
        cost_estimate=pl.CostEstimate(flops=1_073_741_824, bytes_accessed=6_291_456, transcendentals=0),
        compiler_params=BIG,
    )(*pieces, train)


def block_places(half, core):
    x_first, x_second = [jnp.where(core == 0, near("x", 0)[step], near("x", 1)[step]) for step in range(2)]
    z_first, z_second = [jnp.where(core == 0, near("z", 0)[step], near("z", 1)[step]) for step in range(2)]
    x = lax.axis_index("x")
    z = lax.axis_index("zl") ^ (z_second if half else 0)
    z1 = jnp.where((z & 1) == lax.axis_index("c"), z, z ^ z_first) >> 1
    places = []
    for x_base in (x, x ^ x_second):
        for parity in range(2):
            x_of = jnp.where((x_base & 1) == parity, x_base, x_base ^ x_first)
            places += [((2 * zh + z1) * 4 + x_of, yl) for yl in range(2) for zh in range(2)]
    return places


def combine_kernel(keep_0_ref, keep_1_ref, got_0_ref, got_1_ref, out_ref, own_ref, total):
    core = lax.axis_index("c")
    for half, keep_ref in enumerate((keep_0_ref, keep_1_ref)):
        for block, (place, yl) in enumerate(block_places(half, core)):
            total[place, yl * 8 : yl * 8 + 8] = keep_ref[block * 8 : block * 8 + 8]
    for half, got_ref in enumerate((got_0_ref, got_1_ref)):
        for block, (place, yl) in enumerate(block_places(half, 1 - core)):
            rows = slice(yl * 8, yl * 8 + 8)
            total[place, rows] = total[place, rows] + got_ref[1 - core, block * 8 : block * 8 + 8]
    out_ref[...] = total[...].astype(jnp.bfloat16)
    own_ref[...] = total[pl.ds(lax.axis_index("yh") * 4, 4)]


def combine(keeps, gots):
    return pl.pallas_call(
        combine_kernel,
        out_shape=(
            jax.ShapeDtypeStruct((16, 16, 512), jnp.bfloat16),
            jax.ShapeDtypeStruct((4, 16, 512), jnp.float32),
        ),
        in_specs=[WHOLE] * 4,
        out_specs=(WHOLE, WHOLE),
        scratch_shapes=[pltpu.VMEM((16, 16, 512), jnp.float32)],
        cost_estimate=pl.CostEstimate(flops=262_144, bytes_accessed=2_000_000, transcendentals=0),
        compiler_params=SMALL,
    )(*keeps, *gots)


def sum_kernel(parts_ref, own_ref, out_ref):
    chip = lax.axis_index("yh")
    for x in range(4):
        total = own_ref[x]
        for step in range(1, 4):
            total = total + parts_ref[(chip + step) & 3, x].astype(jnp.float32)
        out_ref[x * 8 : x * 8 + 8] = total[:8]
        out_ref[32 + x * 8 : 40 + x * 8] = total[8:]


def final_sum(parts, own):
    return pl.pallas_call(
        sum_kernel,
        out_shape=jax.ShapeDtypeStruct((64, 512), jnp.float32),
        in_specs=[WHOLE] * 2,
        out_specs=WHOLE,
        cost_estimate=pl.CostEstimate(flops=131_072, bytes_accessed=500_000, transcendentals=0),
        compiler_params=SMALL,
    )(parts, own)


def body(train_grads, query_grads, out_inv, in_inv):
    copies, own, factor = prepare(query_grads, out_inv, in_inv)
    raw = lax.all_gather(lax.all_to_all(copies, "yh", 0, 0, tiled=True), "c")
    pre = precondition(raw, own, factor).reshape(8, 32, 128)
    pre = lax.all_gather(pre, "zh")
    held = pre.reshape(16, 4096)
    train = flatten(train_grads.reshape(512, 32, 128))
    square = lax.all_to_all(
        jnp.broadcast_to(held[None], (8,) + held.shape), NAMES, 0, 0, tiled=True, axis_index_groups=square_groups()
    ).reshape(128, 4096)
    first, second = square[:64], square[64:]
    x_first, z_second = exchange(first, True), exchange(second, False)
    x_second, z_first = exchange(second, True), exchange(first, False)
    both_first, both_second = exchange(x_first, False), exchange(z_second, True)

    keep_0, send_0 = half_scores((square, x_first, x_second), train)
    got_0 = lax.all_gather(send_0, "c")
    keep_1, send_1 = half_scores((z_first, z_second, both_first, both_second), train)
    got_1 = lax.all_gather(send_1, "c")
    chip_sum, own_sum = combine((keep_0, keep_1), (got_0, got_1))
    parts = lax.all_to_all(chip_sum.reshape(4, 4, 16, 512), "yh", 0, 0, tiled=True)
    return final_sum(parts, own_sum).T


def solution(mesh):
    fine = Mesh(mesh.devices.reshape(SIZES), NAMES)
    rows, feat = ("zh", "zl", "yl", "x"), ("yh", "c")
    placed = (P(rows, None, feat, None), P(rows, None, feat, None), P(), P())
    return jax.shard_map(
        body, mesh=fine, in_specs=placed, out_specs=P(rows, feat), check_vma=False
    )
```

```python
import itertools

import jax
import jax.numpy as jnp
from jax import lax
from jax.experimental import pallas as pl
from jax.experimental.pallas import tpu as pltpu
from jax.sharding import Mesh
from jax.sharding import PartitionSpec as P

NAMES = ("zh", "zl", "yl", "x", "yh", "c")
SIZES = (2, 4, 2, 4, 4, 2)
WHOLE = pl.BlockSpec(memory_space=pltpu.VMEM)
BIG = pltpu.CompilerParams(vmem_limit_bytes=24 * 1024 * 1024)
SMALL = pltpu.CompilerParams(vmem_limit_bytes=12 * 1024 * 1024)


def near(core):
    return (3, 1) if core == 0 else (1, 3)


def device_index(zh, zl, yl, x, yh, c):
    index = 0
    for size, at in zip(SIZES, (zh, zl, yl, x, yh, c)):
        index = index * size + at
    return index


def z_neighbour(z, mask):
    return z ^ 1 if mask == 1 else (z + (1 if z % 2 else -1)) % 8


def every_device():
    return itertools.product(range(8), range(2), range(4), range(4), range(2))


def square_groups():
    groups = {}
    for z, yl, x, yh, c in every_device():
        x_pair, z_pair = (x, x ^ near(c)[0]), (z, z_neighbour(z, near(c)[0]))
        by_parity = lambda pair: sorted(pair, key=lambda at: at % 2)
        corners = [(z2, x2) for z2 in by_parity(z_pair) for x2 in by_parity(x_pair)]
        groups[tuple(device_index(z2 // 4, z2 % 4, y2, x2, yh, c) for z2, x2 in corners for y2 in range(2))] = None
    return [list(group) for group in groups]


def step_pairs(along_x):
    pairs = []
    for z, yl, x, yh, c in every_device():
        z2, x2 = (z, x ^ near(c)[1]) if along_x else (z_neighbour(z, near(c)[1]), x)
        pairs.append((device_index(z // 4, z % 4, yl, x, yh, c), device_index(z2 // 4, z2 % 4, yl, x2, yh, c)))
    return pairs


def exchange(block, along_x):
    return lax.ppermute(block, NAMES, step_pairs(along_x))


def three_parts(value):
    top = value.astype(jnp.bfloat16)
    rest = value - top.astype(jnp.float32)
    middle = rest.astype(jnp.bfloat16)
    low = (rest - middle.astype(jnp.float32)).astype(jnp.bfloat16)
    return jnp.concatenate([top, middle, low])


def prepare_kernel(query_ref, out_inv_ref, in_inv_ref, copies_ref, own_ref, factor_ref, sems):
    feat = lax.axis_index("yh") * 2 + lax.axis_index("c")
    moves = [pltpu.make_async_copy(query_ref, copies_ref.at[copy], sems.at[copy]) for copy in range(4)]
    own_rows = out_inv_ref.at[:, pl.ds(pl.multiple_of(feat * 16, 16), 16), :]
    moves.append(pltpu.make_async_copy(own_rows, own_ref, sems.at[4]))
    moves.append(pltpu.make_async_copy(in_inv_ref, factor_ref, sems.at[5]))
    for move in moves:
        move.start()
    for move in moves:
        move.wait()


def prepare(queries, out_inv, in_inv):
    far = pl.BlockSpec(memory_space=pltpu.HBM)
    return pl.pallas_call(
        prepare_kernel,
        out_shape=(
            jax.ShapeDtypeStruct((4,) + queries.shape, jnp.bfloat16),
            jax.ShapeDtypeStruct((2, 16, 128), jnp.float32),
            jax.ShapeDtypeStruct((2, 128, 128), jnp.float32),
        ),
        in_specs=[far] * 3,
        out_specs=(WHOLE,) * 3,
        scratch_shapes=[pltpu.SemaphoreType.DMA((6,))],
        cost_estimate=pl.CostEstimate(flops=0, bytes_accessed=700_000, transcendentals=0),
        compiler_params=SMALL,
    )(*(pltpu.with_memory_space_constraint(each, pltpu.HBM) for each in (queries, out_inv, in_inv)))


def precond_kernel(raw_ref, own_ref, in_inv_ref, pre_ref):
    for layer in range(2):
        own = three_parts(own_ref[layer])
        mixed = []
        for q in range(8):
            whole = jnp.concatenate([raw_ref[f % 2, f // 2, q, layer] for f in range(8)])
            parts = jnp.dot(own, whole, preferred_element_type=jnp.float32)
            mixed.append((parts[32:] + parts[16:32]) + parts[:16])
        rows = jnp.dot(
            jnp.concatenate(mixed),
            in_inv_ref[layer],
            precision=lax.Precision.HIGHEST,
            preferred_element_type=jnp.float32,
        )
        pre_ref[:, layer] = rows.astype(jnp.bfloat16).reshape(8, 16, 128)


def precondition(raw, own, in_inv):
    return pl.pallas_call(
        precond_kernel,
        out_shape=jax.ShapeDtypeStruct((8, 2, 16, 128), jnp.bfloat16),
        in_specs=[WHOLE] * 3,
        out_specs=WHOLE,
        cost_estimate=pl.CostEstimate(flops=100_000_000, bytes_accessed=1_000_000, transcendentals=0),
        compiler_params=SMALL,
    )(raw, own, in_inv)


def flatten_kernel(train_ref, flat_ref, held, sems):
    parts = 8
    rows = held.shape[0] // parts
    moves = []
    for part in range(parts):
        window = pl.ds(part * rows, rows)
        moves.append(pltpu.make_async_copy(train_ref.at[window], held.at[window], sems.at[part]))
        moves[part].start()
    for part in range(parts):
        moves[part].wait()
        window = pl.ds(part * rows, rows)
        flat_ref[window, :] = held[window].reshape(rows, 4096)


def flatten(train):
    return pl.pallas_call(
        flatten_kernel,
        out_shape=jax.ShapeDtypeStruct((512, 4096), jnp.bfloat16),
        in_specs=[pl.BlockSpec(memory_space=pltpu.HBM)],
        out_specs=WHOLE,
        scratch_shapes=[pltpu.VMEM((512, 32, 128), jnp.bfloat16), pltpu.SemaphoreType.DMA((8,))],
        cost_estimate=pl.CostEstimate(flops=0, bytes_accessed=8_388_608, transcendentals=0),
        compiler_params=BIG,
    )(pltpu.with_memory_space_constraint(train, pltpu.HBM))


def nt_dot(a, b):
    return lax.dot_general(a, b, (((1,), (1,)), ((), ())), preferred_element_type=jnp.float32)


def split_rows(pieces, keep_ref, send_ref):
    core = lax.axis_index("c")
    for index, (piece, base) in enumerate(pieces):
        rows = slice(index * 64, index * 64 + 64)
        keep_ref[rows] = piece[pl.ds(pl.multiple_of(base + core * 64, 64), 64), :]
        send_ref[rows] = piece[pl.ds(pl.multiple_of(base + 64 - core * 64, 64), 64), :]


def score_kernel(*refs):
    *pieces, train_ref, keep_ref, send_ref, scores = refs
    scores[...] = nt_dot(jnp.concatenate([piece[...] for piece in pieces]), train_ref[...])
    split_rows(((scores, 0), (scores, 128)), keep_ref, send_ref)


def half_scores(pieces, train):
    half = jax.ShapeDtypeStruct((128, 512), jnp.float32)
    return pl.pallas_call(
        score_kernel,
        out_shape=(half, half),
        in_specs=[WHOLE] * (len(pieces) + 1),
        out_specs=(WHOLE, WHOLE),
        scratch_shapes=[pltpu.VMEM((256, 512), jnp.float32)],
        cost_estimate=pl.CostEstimate(flops=1_073_741_824, bytes_accessed=6_291_456, transcendentals=0),
        compiler_params=BIG,
    )(*pieces, train)


def block_places(half, core):
    first, second = [jnp.where(core == 0, near(0)[step], near(1)[step]) for step in range(2)]
    x = lax.axis_index("x")
    z = lax.axis_index("zl") ^ (second if half else 0)
    z1 = jnp.where((z & 1) == lax.axis_index("c"), z, z ^ first) >> 1
    places = []
    for x_base in (x, x ^ second):
        for parity in range(2):
            x_of = jnp.where((x_base & 1) == parity, x_base, x_base ^ first)
            places += [((2 * zh + z1) * 4 + x_of, yl) for yl in range(2) for zh in range(2)]
    return places


def combine_kernel(keep_0_ref, keep_1_ref, got_0_ref, got_1_ref, out_ref, own_ref, total):
    core = lax.axis_index("c")
    for half, keep_ref in enumerate((keep_0_ref, keep_1_ref)):
        for block, (place, yl) in enumerate(block_places(half, core)):
            total[place, yl * 8 : yl * 8 + 8] = keep_ref[block * 8 : block * 8 + 8]
    for half, got_ref in enumerate((got_0_ref, got_1_ref)):
        for block, (place, yl) in enumerate(block_places(half, 1 - core)):
            rows = slice(yl * 8, yl * 8 + 8)
            total[place, rows] = total[place, rows] + got_ref[1 - core, block * 8 : block * 8 + 8]
    out_ref[...] = total[...].astype(jnp.bfloat16)
    own_ref[...] = total[pl.ds(lax.axis_index("yh") * 4, 4)]


def combine(keeps, gots):
    return pl.pallas_call(
        combine_kernel,
        out_shape=(
            jax.ShapeDtypeStruct((16, 16, 512), jnp.bfloat16),
            jax.ShapeDtypeStruct((4, 16, 512), jnp.float32),
        ),
        in_specs=[WHOLE] * 4,
        out_specs=(WHOLE, WHOLE),
        scratch_shapes=[pltpu.VMEM((16, 16, 512), jnp.float32)],
        cost_estimate=pl.CostEstimate(flops=262_144, bytes_accessed=2_000_000, transcendentals=0),
        compiler_params=SMALL,
    )(*keeps, *gots)


def sum_kernel(parts_ref, own_ref, out_ref):
    chip = lax.axis_index("yh")
    for x in range(4):
        total = own_ref[x]
        for step in range(1, 4):
            total = total + parts_ref[(chip + step) & 3, x].astype(jnp.float32)
        out_ref[x * 8 : x * 8 + 8] = total[:8]
        out_ref[32 + x * 8 : 40 + x * 8] = total[8:]


def final_sum(parts, own):
    return pl.pallas_call(
        sum_kernel,
        out_shape=jax.ShapeDtypeStruct((64, 512), jnp.float32),
        in_specs=[WHOLE] * 2,
        out_specs=WHOLE,
        cost_estimate=pl.CostEstimate(flops=131_072, bytes_accessed=500_000, transcendentals=0),
        compiler_params=SMALL,
    )(parts, own)


def body(train_grads, query_grads, out_inv, in_inv):
    copies, own, factor = prepare(query_grads, out_inv, in_inv)
    raw = lax.all_gather(lax.all_to_all(copies, "yh", 0, 0, tiled=True), "c")
    pre = precondition(raw, own, factor).reshape(8, 32, 128)
    pre = lax.all_gather(pre, "zh")
    held = pre.reshape(16, 4096)
    train = flatten(train_grads.reshape(512, 32, 128))
    square = lax.all_to_all(
        jnp.broadcast_to(held[None], (8,) + held.shape), NAMES, 0, 0, tiled=True, axis_index_groups=square_groups()
    ).reshape(128, 4096)
    first, second = square[:64], square[64:]
    x_first, z_second = exchange(first, True), exchange(second, False)
    x_second, z_first = exchange(second, True), exchange(first, False)
    both_first, both_second = exchange(x_first, False), exchange(z_second, True)

    keep_0, send_0 = half_scores((square, x_first, x_second), train)
    got_0 = lax.all_gather(send_0, "c")
    keep_1, send_1 = half_scores((z_first, z_second, both_first, both_second), train)
    got_1 = lax.all_gather(send_1, "c")
    chip_sum, own_sum = combine((keep_0, keep_1), (got_0, got_1))
    parts = lax.all_to_all(chip_sum.reshape(4, 4, 16, 512), "yh", 0, 0, tiled=True)
    return final_sum(parts, own_sum).T


def solution(mesh):
    fine = Mesh(mesh.devices.reshape(SIZES), NAMES)
    rows, feat = ("zh", "zl", "yl", "x"), ("yh", "c")
    placed = (P(rows, None, feat, None), P(rows, None, feat, None), P(), P())
    return jax.shard_map(
        body, mesh=fine, in_specs=placed, out_specs=P(rows, feat), check_vma=False
    )
```

```python
import itertools

import jax
import jax.numpy as jnp
from jax import lax
from jax.experimental import pallas as pl
from jax.experimental.pallas import tpu as pltpu
from jax.sharding import Mesh
from jax.sharding import PartitionSpec as P

NAMES = ("zh", "zl", "yl", "x", "yh", "c")
SIZES = (2, 4, 2, 4, 4, 2)
WHOLE = pl.BlockSpec(memory_space=pltpu.VMEM)
BIG = pltpu.CompilerParams(vmem_limit_bytes=24 * 1024 * 1024)
SMALL = pltpu.CompilerParams(vmem_limit_bytes=12 * 1024 * 1024)


def near(core):
    return (3, 1) if core == 0 else (1, 3)


def device_index(zh, zl, yl, x, yh, c):
    index = 0
    for size, at in zip(SIZES, (zh, zl, yl, x, yh, c)):
        index = index * size + at
    return index


def z_neighbour(z, mask):
    return z ^ 1 if mask == 1 else (z + (1 if z % 2 else -1)) % 8


def every_device():
    return itertools.product(range(8), range(2), range(4), range(4), range(2))


def square_groups():
    groups = {}
    for z, yl, x, yh, c in every_device():
        x_pair, z_pair = (x, x ^ near(c)[0]), (z, z_neighbour(z, near(c)[0]))
        by_parity = lambda pair: sorted(pair, key=lambda at: at % 2)
        corners = [(z2, x2) for z2 in by_parity(z_pair) for x2 in by_parity(x_pair)]
        groups[tuple(device_index(z2 // 4, z2 % 4, y2, x2, yh, c) for z2, x2 in corners for y2 in range(2))] = None
    return [list(group) for group in groups]


def step_pairs(along_x):
    pairs = []
    for z, yl, x, yh, c in every_device():
        z2, x2 = (z, x ^ near(c)[1]) if along_x else (z_neighbour(z, near(c)[1]), x)
        pairs.append((device_index(z // 4, z % 4, yl, x, yh, c), device_index(z2 // 4, z2 % 4, yl, x2, yh, c)))
    return pairs


def exchange(block, along_x):
    return lax.ppermute(block, NAMES, step_pairs(along_x))


def three_parts(value):
    top = value.astype(jnp.bfloat16)
    rest = value - top.astype(jnp.float32)
    middle = rest.astype(jnp.bfloat16)
    low = (rest - middle.astype(jnp.float32)).astype(jnp.bfloat16)
    return jnp.concatenate([top, middle, low])


def prepare_kernel(query_ref, out_inv_ref, in_inv_ref, copies_ref, own_ref, factor_ref, sems):
    feat = lax.axis_index("yh") * 2 + lax.axis_index("c")
    moves = [pltpu.make_async_copy(query_ref, copies_ref.at[copy], sems.at[copy]) for copy in range(4)]
    own_rows = out_inv_ref.at[:, pl.ds(pl.multiple_of(feat * 16, 16), 16), :]
    moves.append(pltpu.make_async_copy(own_rows, own_ref, sems.at[4]))
    moves.append(pltpu.make_async_copy(in_inv_ref, factor_ref, sems.at[5]))
    for move in moves:
        move.start()
    for move in moves:
        move.wait()


def prepare(queries, out_inv, in_inv):
    far = pl.BlockSpec(memory_space=pltpu.HBM)
    return pl.pallas_call(
        prepare_kernel,
        out_shape=(
            jax.ShapeDtypeStruct((4,) + queries.shape, jnp.bfloat16),
            jax.ShapeDtypeStruct((2, 16, 128), jnp.float32),
            jax.ShapeDtypeStruct((2, 128, 128), jnp.float32),
        ),
        in_specs=[far] * 3,
        out_specs=(WHOLE,) * 3,
        scratch_shapes=[pltpu.SemaphoreType.DMA((6,))],
        cost_estimate=pl.CostEstimate(flops=0, bytes_accessed=700_000, transcendentals=0),
        compiler_params=SMALL,
    )(*(pltpu.with_memory_space_constraint(each, pltpu.HBM) for each in (queries, out_inv, in_inv)))


def precond_kernel(raw_ref, own_ref, in_inv_ref, pre_ref):
    for layer in range(2):
        own = three_parts(own_ref[layer])
        mixed = []
        for q in range(8):
            whole = jnp.concatenate([raw_ref[f % 2, f // 2, q, layer] for f in range(8)])
            parts = jnp.dot(own, whole, preferred_element_type=jnp.float32)
            mixed.append((parts[32:] + parts[16:32]) + parts[:16])
        rows = jnp.dot(
            jnp.concatenate(mixed),
            in_inv_ref[layer],
            precision=lax.Precision.HIGHEST,
            preferred_element_type=jnp.float32,
        )
        pre_ref[:, layer] = rows.astype(jnp.bfloat16).reshape(8, 16, 128)


def precondition(raw, own, in_inv):
    return pl.pallas_call(
        precond_kernel,
        out_shape=jax.ShapeDtypeStruct((8, 2, 16, 128), jnp.bfloat16),
        in_specs=[WHOLE] * 3,
        out_specs=WHOLE,
        cost_estimate=pl.CostEstimate(flops=100_000_000, bytes_accessed=1_000_000, transcendentals=0),
        compiler_params=SMALL,
    )(raw, own, in_inv)


def flatten_kernel(train_ref, flat_ref, held, sems):
    parts = 8
    rows = held.shape[0] // parts
    moves = []
    for part in range(parts):
        window = pl.ds(part * rows, rows)
        moves.append(pltpu.make_async_copy(train_ref.at[window], held.at[window], sems.at[part]))
        moves[part].start()
    for part in range(parts):
        moves[part].wait()
        window = pl.ds(part * rows, rows)
        flat_ref[window, :] = held[window].reshape(rows, 4096)


def flatten(train):
    return pl.pallas_call(
        flatten_kernel,
        out_shape=jax.ShapeDtypeStruct((512, 4096), jnp.bfloat16),
        in_specs=[pl.BlockSpec(memory_space=pltpu.HBM)],
        out_specs=WHOLE,
        scratch_shapes=[pltpu.VMEM((512, 32, 128), jnp.bfloat16), pltpu.SemaphoreType.DMA((8,))],
        cost_estimate=pl.CostEstimate(flops=0, bytes_accessed=8_388_608, transcendentals=0),
        compiler_params=BIG,
    )(pltpu.with_memory_space_constraint(train, pltpu.HBM))


def nt_dot(a, b):
    return lax.dot_general(a, b, (((1,), (1,)), ((), ())), preferred_element_type=jnp.float32)


def split_rows(pieces, keep_ref, send_ref):
    core = lax.axis_index("c")
    for index, (piece, base) in enumerate(pieces):
        rows = slice(index * 64, index * 64 + 64)
        keep_ref[rows] = piece[pl.ds(pl.multiple_of(base + core * 64, 64), 64), :]
        send_ref[rows] = piece[pl.ds(pl.multiple_of(base + 64 - core * 64, 64), 64), :]


def score_kernel(*refs):
    *pieces, train_ref, keep_ref, send_ref, scores = refs
    scores[...] = nt_dot(jnp.concatenate([piece[...] for piece in pieces]), train_ref[...])
    split_rows(((scores, 0), (scores, 128)), keep_ref, send_ref)


def half_scores(pieces, train):
    half = jax.ShapeDtypeStruct((128, 512), jnp.float32)
    return pl.pallas_call(
        score_kernel,
        out_shape=(half, half),
        in_specs=[WHOLE] * (len(pieces) + 1),
        out_specs=(WHOLE, WHOLE),
        scratch_shapes=[pltpu.VMEM((256, 512), jnp.float32)],
        cost_estimate=pl.CostEstimate(flops=1_073_741_824, bytes_accessed=6_291_456, transcendentals=0),
        compiler_params=BIG,
    )(*pieces, train)


def block_places(half, core):
    first, second = [jnp.where(core == 0, near(0)[step], near(1)[step]) for step in range(2)]
    x = lax.axis_index("x")
    z = lax.axis_index("zl") ^ (second if half else 0)
    z1 = jnp.where((z & 1) == lax.axis_index("c"), z, z ^ first) >> 1
    places = []
    for x_base in (x, x ^ second):
        for parity in range(2):
            x_of = jnp.where((x_base & 1) == parity, x_base, x_base ^ first)
            places += [((2 * zh + z1) * 4 + x_of, yl) for yl in range(2) for zh in range(2)]
    return places


def combine_kernel(keep_0_ref, keep_1_ref, got_0_ref, got_1_ref, out_ref, own_ref, total):
    core = lax.axis_index("c")
    for half, keep_ref in enumerate((keep_0_ref, keep_1_ref)):
        for block, (place, yl) in enumerate(block_places(half, core)):
            total[place, yl * 8 : yl * 8 + 8] = keep_ref[block * 8 : block * 8 + 8]
    for half, got_ref in enumerate((got_0_ref, got_1_ref)):
        for block, (place, yl) in enumerate(block_places(half, 1 - core)):
            rows = slice(yl * 8, yl * 8 + 8)
            total[place, rows] = total[place, rows] + got_ref[1 - core, block * 8 : block * 8 + 8]
    out_ref[...] = total[...].astype(jnp.bfloat16)
    own_ref[...] = total[pl.ds(lax.axis_index("yh") * 4, 4)]


def combine(keeps, gots):
    return pl.pallas_call(
        combine_kernel,
        out_shape=(
            jax.ShapeDtypeStruct((16, 16, 512), jnp.bfloat16),
            jax.ShapeDtypeStruct((4, 16, 512), jnp.float32),
        ),
        in_specs=[WHOLE] * 4,
        out_specs=(WHOLE, WHOLE),
        scratch_shapes=[pltpu.VMEM((16, 16, 512), jnp.float32)],
        cost_estimate=pl.CostEstimate(flops=262_144, bytes_accessed=2_000_000, transcendentals=0),
        compiler_params=SMALL,
    )(*keeps, *gots)


def sum_kernel(parts_ref, own_ref, out_ref):
    chip = lax.axis_index("yh")
    for x in range(4):
        total = own_ref[x]
        for step in range(1, 4):
            total = total + parts_ref[(chip + step) & 3, x].astype(jnp.float32)
        out_ref[x * 8 : x * 8 + 8] = total[:8]
        out_ref[32 + x * 8 : 40 + x * 8] = total[8:]


def final_sum(parts, own):
    return pl.pallas_call(
        sum_kernel,
        out_shape=jax.ShapeDtypeStruct((64, 512), jnp.float32),
        in_specs=[WHOLE] * 2,
        out_specs=WHOLE,
        cost_estimate=pl.CostEstimate(flops=131_072, bytes_accessed=500_000, transcendentals=0),
        compiler_params=SMALL,
    )(parts, own)


def body(train_grads, query_grads, out_inv, in_inv):
    copies, own, factor = prepare(query_grads, out_inv, in_inv)
    raw = lax.all_gather(lax.all_to_all(copies, "yh", 0, 0, tiled=True), "c")
    pre = precondition(raw, own, factor).reshape(8, 32, 128)
    pre = lax.all_gather(pre, "zh")
    held = pre.reshape(16, 4096)
    train = flatten(train_grads.reshape(512, 32, 128))
    square = lax.all_to_all(
        jnp.broadcast_to(held[None], (8,) + held.shape), NAMES, 0, 0, tiled=True, axis_index_groups=square_groups()
    ).reshape(128, 4096)
    first, second = square[:64], square[64:]
    z_first, x_second = exchange(first, False), exchange(second, True)
    z_second, x_first = exchange(second, False), exchange(first, True)
    both_first, both_second = exchange(z_first, True), exchange(x_second, False)

    keep_0, send_0 = half_scores((square, x_first, x_second), train)
    got_0 = lax.all_gather(send_0, "c")
    keep_1, send_1 = half_scores((z_first, z_second, both_first, both_second), train)
    got_1 = lax.all_gather(send_1, "c")
    chip_sum, own_sum = combine((keep_0, keep_1), (got_0, got_1))
    parts = lax.all_to_all(chip_sum.reshape(4, 4, 16, 512), "yh", 0, 0, tiled=True)
    return final_sum(parts, own_sum).T


def solution(mesh):
    fine = Mesh(mesh.devices.reshape(SIZES), NAMES)
    rows, feat = ("zh", "zl", "yl", "x"), ("yh", "c")
    placed = (P(rows, None, feat, None), P(rows, None, feat, None), P(), P())
    return jax.shard_map(
        body, mesh=fine, in_specs=placed, out_specs=P(rows, feat), check_vma=False
    )
```

```python
import itertools

import jax
import jax.numpy as jnp
from jax import lax
from jax.experimental import pallas as pl
from jax.experimental.pallas import tpu as pltpu
from jax.sharding import Mesh
from jax.sharding import PartitionSpec as P

NAMES = ("zh", "zl", "yl", "x", "yh", "c")
SIZES = (2, 4, 2, 4, 4, 2)
WHOLE = pl.BlockSpec(memory_space=pltpu.VMEM)
BIG = pltpu.CompilerParams(vmem_limit_bytes=24 * 1024 * 1024)
SMALL = pltpu.CompilerParams(vmem_limit_bytes=12 * 1024 * 1024)


def near(core):
    return (3, 1) if core == 0 else (1, 3)


def device_index(zh, zl, yl, x, yh, c):
    index = 0
    for size, at in zip(SIZES, (zh, zl, yl, x, yh, c)):
        index = index * size + at
    return index


def z_neighbour(z, mask):
    return z ^ 1 if mask == 1 else (z + (1 if z % 2 else -1)) % 8


def every_device():
    return itertools.product(range(8), range(2), range(4), range(4), range(2))


def square_groups():
    groups = {}
    for z, yl, x, yh, c in every_device():
        x_pair, z_pair = (x, x ^ near(c)[0]), (z, z_neighbour(z, near(c)[0]))
        by_parity = lambda pair: sorted(pair, key=lambda at: at % 2)
        corners = [(z2, x2) for z2 in by_parity(z_pair) for x2 in by_parity(x_pair)]
        groups[tuple(device_index(z2 // 4, z2 % 4, y2, x2, yh, c) for z2, x2 in corners for y2 in range(2))] = None
    return [list(group) for group in groups]


def step_pairs(way):
    pairs = []
    for z, yl, x, yh, c in every_device():
        along_x = way == c
        z2, x2 = (z, x ^ near(c)[1]) if along_x else (z_neighbour(z, near(c)[1]), x)
        pairs.append((device_index(z // 4, z % 4, yl, x, yh, c), device_index(z2 // 4, z2 % 4, yl, x2, yh, c)))
    return pairs


def exchange(block, way):
    return lax.ppermute(block, NAMES, step_pairs(way))


def three_parts(value):
    top = value.astype(jnp.bfloat16)
    rest = value - top.astype(jnp.float32)
    middle = rest.astype(jnp.bfloat16)
    low = (rest - middle.astype(jnp.float32)).astype(jnp.bfloat16)
    return jnp.concatenate([top, middle, low])


def prepare_kernel(query_ref, out_inv_ref, in_inv_ref, copies_ref, own_ref, factor_ref, sems):
    feat = lax.axis_index("yh") * 2 + lax.axis_index("c")
    moves = [pltpu.make_async_copy(query_ref, copies_ref.at[copy], sems.at[copy]) for copy in range(4)]
    own_rows = out_inv_ref.at[:, pl.ds(pl.multiple_of(feat * 16, 16), 16), :]
    moves.append(pltpu.make_async_copy(own_rows, own_ref, sems.at[4]))
    moves.append(pltpu.make_async_copy(in_inv_ref, factor_ref, sems.at[5]))
    for move in moves:
        move.start()
    for move in moves:
        move.wait()


def prepare(queries, out_inv, in_inv):
    far = pl.BlockSpec(memory_space=pltpu.HBM)
    return pl.pallas_call(
        prepare_kernel,
        out_shape=(
            jax.ShapeDtypeStruct((4,) + queries.shape, jnp.bfloat16),
            jax.ShapeDtypeStruct((2, 16, 128), jnp.float32),
            jax.ShapeDtypeStruct((2, 128, 128), jnp.float32),
        ),
        in_specs=[far] * 3,
        out_specs=(WHOLE,) * 3,
        scratch_shapes=[pltpu.SemaphoreType.DMA((6,))],
        cost_estimate=pl.CostEstimate(flops=0, bytes_accessed=700_000, transcendentals=0),
        compiler_params=SMALL,
    )(*(pltpu.with_memory_space_constraint(each, pltpu.HBM) for each in (queries, out_inv, in_inv)))


def precond_kernel(raw_ref, own_ref, in_inv_ref, pre_ref):
    for layer in range(2):
        own = three_parts(own_ref[layer])
        mixed = []
        for q in range(8):
            whole = jnp.concatenate([raw_ref[f % 2, f // 2, q, layer] for f in range(8)])
            parts = jnp.dot(own, whole, preferred_element_type=jnp.float32)
            mixed.append((parts[32:] + parts[16:32]) + parts[:16])
        rows = jnp.dot(
            jnp.concatenate(mixed),
            in_inv_ref[layer],
            precision=lax.Precision.HIGHEST,
            preferred_element_type=jnp.float32,
        )
        pre_ref[:, layer] = rows.astype(jnp.bfloat16).reshape(8, 16, 128)


def precondition(raw, own, in_inv):
    return pl.pallas_call(
        precond_kernel,
        out_shape=jax.ShapeDtypeStruct((8, 2, 16, 128), jnp.bfloat16),
        in_specs=[WHOLE] * 3,
        out_specs=WHOLE,
        cost_estimate=pl.CostEstimate(flops=100_000_000, bytes_accessed=1_000_000, transcendentals=0),
        compiler_params=SMALL,
    )(raw, own, in_inv)


def flatten_kernel(train_ref, flat_ref, held, sems):
    parts = 8
    rows = held.shape[0] // parts
    moves = []
    for part in range(parts):
        window = pl.ds(part * rows, rows)
        moves.append(pltpu.make_async_copy(train_ref.at[window], held.at[window], sems.at[part]))
        moves[part].start()
    for part in range(parts):
        moves[part].wait()
        window = pl.ds(part * rows, rows)
        flat_ref[window, :] = held[window].reshape(rows, 4096)


def flatten(train):
    return pl.pallas_call(
        flatten_kernel,
        out_shape=jax.ShapeDtypeStruct((512, 4096), jnp.bfloat16),
        in_specs=[pl.BlockSpec(memory_space=pltpu.HBM)],
        out_specs=WHOLE,
        scratch_shapes=[pltpu.VMEM((512, 32, 128), jnp.bfloat16), pltpu.SemaphoreType.DMA((8,))],
        cost_estimate=pl.CostEstimate(flops=0, bytes_accessed=8_388_608, transcendentals=0),
        compiler_params=BIG,
    )(pltpu.with_memory_space_constraint(train, pltpu.HBM))


def nt_dot(a, b):
    return lax.dot_general(a, b, (((1,), (1,)), ((), ())), preferred_element_type=jnp.float32)


def split_rows(pieces, keep_ref, send_ref):
    core = lax.axis_index("c")
    for index, (piece, base) in enumerate(pieces):
        rows = slice(index * 64, index * 64 + 64)
        keep_ref[rows] = piece[pl.ds(pl.multiple_of(base + core * 64, 64), 64), :]
        send_ref[rows] = piece[pl.ds(pl.multiple_of(base + 64 - core * 64, 64), 64), :]


def score_kernel(*refs):
    *pieces, train_ref, keep_ref, send_ref, scores = refs
    scores[...] = nt_dot(jnp.concatenate([piece[...] for piece in pieces]), train_ref[...])
    split_rows(((scores, 0), (scores, 128)), keep_ref, send_ref)


def half_scores(pieces, train):
    half = jax.ShapeDtypeStruct((128, 512), jnp.float32)
    return pl.pallas_call(
        score_kernel,
        out_shape=(half, half),
        in_specs=[WHOLE] * (len(pieces) + 1),
        out_specs=(WHOLE, WHOLE),
        scratch_shapes=[pltpu.VMEM((256, 512), jnp.float32)],
        cost_estimate=pl.CostEstimate(flops=1_073_741_824, bytes_accessed=6_291_456, transcendentals=0),
        compiler_params=BIG,
    )(*pieces, train)


def block_places(half, core):
    first, second = [jnp.where(core == 0, near(0)[step], near(1)[step]) for step in range(2)]
    x, z = lax.axis_index("x"), lax.axis_index("zl")
    places = []
    for piece in range(2):
        x_far, z_far = jnp.where(core == 0, piece, half), jnp.where(core == 0, half, piece)
        x_base, z_base = x ^ (second * x_far), z ^ (second * z_far)
        z1 = jnp.where((z_base & 1) == lax.axis_index("c"), z_base, z_base ^ first) >> 1
        for parity in range(2):
            x_of = jnp.where((x_base & 1) == parity, x_base, x_base ^ first)
            places += [((2 * zh + z1) * 4 + x_of, yl) for yl in range(2) for zh in range(2)]
    return places


def combine_kernel(keep_0_ref, keep_1_ref, got_0_ref, got_1_ref, out_ref, own_ref, total):
    core = lax.axis_index("c")
    for half, keep_ref in enumerate((keep_0_ref, keep_1_ref)):
        for block, (place, yl) in enumerate(block_places(half, core)):
            total[place, yl * 8 : yl * 8 + 8] = keep_ref[block * 8 : block * 8 + 8]
    for half, got_ref in enumerate((got_0_ref, got_1_ref)):
        for block, (place, yl) in enumerate(block_places(half, 1 - core)):
            rows = slice(yl * 8, yl * 8 + 8)
            total[place, rows] = total[place, rows] + got_ref[1 - core, block * 8 : block * 8 + 8]
    out_ref[...] = total[...].astype(jnp.bfloat16)
    own_ref[...] = total[pl.ds(lax.axis_index("yh") * 4, 4)]


def combine(keeps, gots):
    return pl.pallas_call(
        combine_kernel,
        out_shape=(
            jax.ShapeDtypeStruct((16, 16, 512), jnp.bfloat16),
            jax.ShapeDtypeStruct((4, 16, 512), jnp.float32),
        ),
        in_specs=[WHOLE] * 4,
        out_specs=(WHOLE, WHOLE),
        scratch_shapes=[pltpu.VMEM((16, 16, 512), jnp.float32)],
        cost_estimate=pl.CostEstimate(flops=262_144, bytes_accessed=2_000_000, transcendentals=0),
        compiler_params=SMALL,
    )(*keeps, *gots)


def sum_kernel(parts_ref, own_ref, out_ref):
    chip = lax.axis_index("yh")
    for x in range(4):
        total = own_ref[x]
        for step in range(1, 4):
            total = total + parts_ref[(chip + step) & 3, x].astype(jnp.float32)
        out_ref[x * 8 : x * 8 + 8] = total[:8]
        out_ref[32 + x * 8 : 40 + x * 8] = total[8:]


def final_sum(parts, own):
    return pl.pallas_call(
        sum_kernel,
        out_shape=jax.ShapeDtypeStruct((64, 512), jnp.float32),
        in_specs=[WHOLE] * 2,
        out_specs=WHOLE,
        cost_estimate=pl.CostEstimate(flops=131_072, bytes_accessed=500_000, transcendentals=0),
        compiler_params=SMALL,
    )(parts, own)


def body(train_grads, query_grads, out_inv, in_inv):
    copies, own, factor = prepare(query_grads, out_inv, in_inv)
    raw = lax.all_gather(lax.all_to_all(copies, "yh", 0, 0, tiled=True), "c")
    pre = precondition(raw, own, factor).reshape(8, 32, 128)
    pre = lax.all_gather(pre, "zh")
    held = pre.reshape(16, 4096)
    train = flatten(train_grads.reshape(512, 32, 128))
    square = lax.all_to_all(
        jnp.broadcast_to(held[None], (8,) + held.shape), NAMES, 0, 0, tiled=True, axis_index_groups=square_groups()
    ).reshape(128, 4096)
    first, second = square[:64], square[64:]
    x_first, z_second = exchange(first, 0), exchange(second, 1)
    x_second, z_first = exchange(second, 0), exchange(first, 1)
    both_first, both_second = exchange(x_first, 1), exchange(z_second, 0)

    keep_0, send_0 = half_scores((square, x_first, x_second), train)
    got_0 = lax.all_gather(send_0, "c")
    keep_1, send_1 = half_scores((z_first, z_second, both_first, both_second), train)
    got_1 = lax.all_gather(send_1, "c")
    chip_sum, own_sum = combine((keep_0, keep_1), (got_0, got_1))
    parts = lax.all_to_all(chip_sum.reshape(4, 4, 16, 512), "yh", 0, 0, tiled=True)
    return final_sum(parts, own_sum).T


def solution(mesh):
    fine = Mesh(mesh.devices.reshape(SIZES), NAMES)
    rows, feat = ("zh", "zl", "yl", "x"), ("yh", "c")
    placed = (P(rows, None, feat, None), P(rows, None, feat, None), P(), P())
    return jax.shard_map(
        body, mesh=fine, in_specs=placed, out_specs=P(rows, feat), check_vma=False
    )
```
